32 devices in a mesh: rows: 16 (over z, y, core), chan: 2 (over x).
Axes of the slice: x: 2, y: 2, z: 4, core: 2. Of those that a mesh axis runs over, the one named last changes fastest.
Arguments:
- pair: bfloat16 [128, 128, 128], P('rows', 'chan'), may hold values from -6 to 6
- block_mask: int32 [1, 1], replicated, may hold values from 0 to 1, as said below
- w_in: bfloat16 [128, 640], replicated, may hold values from -0.5 to 0.5
- w_out: bfloat16 [128, 128], replicated, may hold values from -0.5 to 0.5
Outputs:
- update: bfloat16 [128, 128, 128], P('rows', 'chan')
The draws below stay inside these ranges and needn't reach their ends.
Inputs may be any that keep to these rules, and one draw needn't show every extreme that they name: Every diagonal entry of block_mask is 1; other entries are 0 or 1.
All inputs are finite; a program needn't handle non-finite values.
Results may differ from the reference program's by a relative error of at most 0.0078.
Values may be sent and summed in bfloat16 or wider, within the bound.
No kernel may reach another device: no remote copies, remote signals or barrier semaphores. Data moves between devices by JAX's collectives and lax.ppermute only.
A program may use at most 64 MiB of HBM per device.

```python
import jax
import jax.numpy as jnp
from jax import lax

C = 128
BLOCK = 128
TOKENS = 128


def draw_block_mask(key, part):
    blocks = TOKENS // BLOCK
    values = jax.random.randint(key, (blocks, blocks), 0, 10)
    first = lax.broadcasted_iota(jnp.int32, (blocks, blocks), 0)
    second = lax.broadcasted_iota(jnp.int32, (blocks, blocks), 1)
    return jnp.where((first == second) | (values < 3), 1, 0).astype(jnp.int32)


def level_of(rng, extent, split, smallest, largest):
    factor_of, own = 1.0, jax.random.fold_in(rng, 6)
    for axis_at, shards_of in split:
        steps = jnp.exp(jax.random.uniform(jax.random.fold_in(own, axis_at), (shards_of,), jnp.float32, smallest / len(split), largest / len(split)))
        factor_of = factor_of * jnp.repeat(steps, extent[axis_at] // shards_of).reshape([-1 if axis == axis_at else 1 for axis in range(len(extent))])
    return factor_of


def noise(stream_key, extent, spread, reach, shards=(), dtype=jnp.bfloat16):
    values = spread * jax.random.normal(stream_key, extent, jnp.float32)
    if shards:
        values = values * level_of(stream_key, extent, shards, -0.22, 0.18)
    return jnp.clip(values, -reach, reach).astype(dtype)


def setup_inputs(seed: int = 0) -> dict:
    splits = jax.random.split(jax.random.key(seed), 5)
    pair = noise(splits[0], (TOKENS, TOKENS, C), 1.0, 6.0, ((0, 16), (1, 2)))
    block_mask = draw_block_mask(jax.random.fold_in(splits[4], 71), 0)
    w_in = noise(splits[2], (C, 5 * C), C ** -0.5, 0.5)
    w_out = noise(splits[3], (C, C), C ** -0.5, 0.5)
    return {"pair": pair, "block_mask": block_mask, "w_in": w_in, "w_out": w_out}


def layer_norm(values):
    mean = lax.optimization_barrier(jnp.mean(values, axis=-1, keepdims=True))
    centered = values - mean
    var = lax.optimization_barrier(jnp.mean(centered * centered, axis=-1, keepdims=True))
    return centered / jnp.sqrt(var + 1e-05)

def reference(pair, block_mask, w_in, w_out):
    count = pair.shape[0]
    width = pair.shape[2]
    normed = layer_norm(pair.astype(jnp.float32)).astype(jnp.bfloat16)
    proj = jnp.dot(normed.reshape(-1, width), w_in, preferred_element_type=jnp.float32).reshape(count, count, 5 * width)
    mask = jnp.repeat(jnp.repeat(block_mask.astype(jnp.float32), BLOCK, axis=0), BLOCK, axis=1)[:, :, None]
    left = (jax.nn.sigmoid(proj[..., :width]) * proj[..., width:2 * width] * mask).astype(jnp.bfloat16)
    right = (jax.nn.sigmoid(proj[..., 2 * width:3 * width]) * proj[..., 3 * width:4 * width] * mask).astype(jnp.bfloat16)
    gate = jax.nn.sigmoid(proj[..., 4 * width:])
    left_t = jnp.transpose(left, (2, 0, 1)).astype(jnp.float32)
    right_t = jnp.transpose(right, (2, 0, 1)).astype(jnp.float32)
    prod = jnp.einsum('cik,cjk->cij', left_t, right_t)
    prod = jnp.transpose(prod, (1, 2, 0))
    normed_prod = layer_norm(prod).astype(jnp.bfloat16)
    mixed = jnp.dot(normed_prod.reshape(-1, width), w_out, preferred_element_type=jnp.float32).reshape(count, count, width)
    return (gate * mixed).astype(jnp.bfloat16)
```

```python
import jax
import jax.numpy as jnp
from jax import lax
from jax.experimental import pallas as pl
from jax.experimental.pallas import tpu as pltpu
from jax.sharding import PartitionSpec as P

BLOCK = 128
LANES = 128
SUBLANES = 8
EPS = 1e-05
AXES = ("rows", "chan")


def layer_norm(values):
    mean = jnp.mean(values, axis=-1, keepdims=True)
    centered = values - mean
    var = jnp.mean(centered * centered, axis=-1, keepdims=True)
    return centered / jnp.sqrt(var + EPS)


def channel_product(left, piece):
    return jnp.einsum("cik,cjk->cij", left, piece, preferred_element_type=jnp.float32)


def gathered(pair, block_mask, w_in, w_out):
    rows_dev, cols_dev, width = pair.shape
    n_blocks = block_mask.shape[0]
    row_start = lax.axis_index("rows") * rows_dev
    col_start = lax.axis_index("chan") * cols_dev
    row_ids = row_start + lax.broadcasted_iota(jnp.int32, (rows_dev, n_blocks), 0)
    col_ids = col_start + lax.broadcasted_iota(jnp.int32, (cols_dev, n_blocks), 0)
    rows_hot = (
        row_ids // BLOCK == lax.broadcasted_iota(jnp.int32, (rows_dev, n_blocks), 1)
    ).astype(jnp.float32)
    cols_hot = (
        col_ids // BLOCK == lax.broadcasted_iota(jnp.int32, (cols_dev, n_blocks), 1)
    ).astype(jnp.float32)
    mask_float = block_mask.astype(jnp.float32)
    local_mask = jnp.dot(jnp.dot(rows_hot, mask_float), cols_hot.T)[:, :, None]
    normed = layer_norm(pair.astype(jnp.float32)).astype(jnp.bfloat16)
    proj = jnp.dot(normed.reshape(-1, width), w_in, preferred_element_type=jnp.float32).reshape(
        rows_dev, cols_dev, 5 * width
    )
    left = (jax.nn.sigmoid(proj[..., :width]) * proj[..., width : 2 * width] * local_mask).astype(
        jnp.bfloat16
    )
    right = (
        jax.nn.sigmoid(proj[..., 2 * width : 3 * width])
        * proj[..., 3 * width : 4 * width]
        * local_mask
    ).astype(jnp.bfloat16)
    gate = jax.nn.sigmoid(proj[..., 4 * width :])
    left_t = jnp.transpose(left, (2, 0, 1))
    right_t = jnp.transpose(right, (2, 0, 1))
    left_ch, right_ch = (
        lax.all_to_all(left_t, "chan", split_axis=0, concat_axis=2, tiled=True),
        lax.all_to_all(right_t, "chan", split_axis=0, concat_axis=2, tiled=True),
    )
    prod_ch = channel_product(left_ch, lax.all_gather(right_ch, "rows", axis=1, tiled=True))
    prod_back = lax.all_to_all(prod_ch, "chan", split_axis=2, concat_axis=0, tiled=True)
    prod = jnp.transpose(prod_back, (1, 2, 0))
    normed_prod = layer_norm(prod).astype(jnp.bfloat16)
    mixed = jnp.dot(
        normed_prod.reshape(-1, width), w_out, preferred_element_type=jnp.float32
    ).reshape(rows_dev, cols_dev, width)
    return (gate * mixed).astype(jnp.bfloat16)


def dot_t(a, b, contract):
    return lax.dot_general(a, b, ((contract[:1], contract[1:]), ((), ())), preferred_element_type=jnp.float32)


def first_half(shape):
    return lax.broadcasted_iota(jnp.int32, shape, len(shape) - 1) < LANES // 2


def swap(values):
    return pltpu.roll(values, LANES // 2, values.ndim - 1)


def project_kernel(mask_ref, pair_ref, w_ref, out_ref, gate_ref, parts):
    rows_dev, cols_dev, width = pair_ref.shape
    tokens, half = rows_dev * cols_dev, width // 2
    row_block = lax.axis_index("rows") * rows_dev // BLOCK
    col_block = lax.axis_index("chan") * cols_dev // BLOCK
    half_mask = 0.5 * mask_ref[row_block, col_block].astype(jnp.float32)

    pair = pair_ref[...].reshape(tokens, width)
    ones = jnp.ones((width, width), jnp.bfloat16)
    mean = jnp.dot(pair, ones, preferred_element_type=jnp.float32) * (1.0 / width)
    centered = pair.astype(jnp.float32) - mean
    square = centered * centered
    high = square.astype(jnp.bfloat16)
    low = (square - high.astype(jnp.float32)).astype(jnp.bfloat16)
    total = jnp.dot(high, ones, preferred_element_type=jnp.float32) + jnp.dot(
        low, ones, preferred_element_type=jnp.float32
    )
    normed = (centered * lax.rsqrt(total * (1.0 / width) + EPS)).astype(jnp.bfloat16)

    pick = first_half((half, LANES))
    for side in range(2):
        begin = 2 * side * width
        gates = dot_t(w_ref[:, begin : begin + width], normed, (0, 1))
        values = dot_t(w_ref[:, begin + width : begin + 2 * width], normed, (0, 1))
        held = (jnp.tanh(0.5 * gates) * half_mask + half_mask) * values
        for at in range(tokens // LANES):
            low_c = held[:half, at * LANES : (at + 1) * LANES]
            high_c = held[half:, at * LANES : (at + 1) * LANES]
            parts[side, :, 2 * at, :] = jnp.where(pick, low_c, swap(high_c))
            parts[side, :, 2 * at + 1, :] = jnp.where(pick, swap(low_c), high_c)
    n_dev, slab = out_ref.shape[0], out_ref.shape[1] // 2
    for side in range(2):
        out_ref[:, side * slab : (side + 1) * slab, :] = (
            parts[side].reshape(n_dev, slab, LANES).astype(jnp.bfloat16)
        )
    gate = jnp.dot(normed, w_ref[:, 4 * width :], preferred_element_type=jnp.float32)
    gate_ref[...] = 0.5 * jnp.tanh(0.5 * gate) + 0.5


def product_kernel(in_ref, out_ref):
    n_rows, n_chan, slabs, _ = in_ref.shape
    slab = slabs // 2
    groups = slab // SUBLANES
    tokens = n_rows * SUBLANES

    def side(at):
        values = in_ref[:, :, at * slab : (at + 1) * slab, :].astype(jnp.float32)
        return values.reshape(n_rows, n_chan, groups, SUBLANES, LANES)

    left, right = side(0), side(1)
    pick = first_half((tokens, LANES))
    made = []
    for g in range(groups):
        a = [left[:, x, g].reshape(tokens, LANES) for x in range(n_chan)]
        b = [right[:, x, g].reshape(tokens, LANES) for x in range(n_chan)]
        rows = [
            jnp.concatenate([jnp.where(pick, v, 0.0) for v in a], axis=1),
            jnp.concatenate([jnp.where(pick, 0.0, v) for v in a], axis=1),
        ]
        a = jnp.concatenate(rows, axis=0).astype(jnp.bfloat16)
        b = jnp.concatenate(b, axis=1).astype(jnp.bfloat16)
        prod = dot_t(a, b, (1, 1))
        made.append((prod[:tokens], prod[tokens:]))
    blocks = [
        [jnp.where(pick, low, swap(high)) for low, high in made],
        [jnp.where(pick, swap(low), high) for low, high in made],
    ]
    for x in range(n_chan):
        block = jnp.concatenate([v.reshape(n_rows, SUBLANES, LANES) for v in blocks[x]], axis=1)
        out_ref[:, x] = block.astype(jnp.bfloat16)


def finish_kernel(prod_ref, gate_ref, w_ref, out_ref, parts):
    n_dev, slab, _ = prod_ref.shape
    rows_dev, cols_dev, width = out_ref.shape
    prod = prod_ref[...].astype(jnp.float32).reshape(n_dev * slab // SUBLANES, SUBLANES, LANES)
    total = jnp.sum(prod, axis=0)
    mean = (total + swap(total)) * (1.0 / width)
    centered = prod - mean
    total = jnp.sum(centered * centered, axis=0)
    var = (total + swap(total)) * (1.0 / width)
    parts[...] = centered * lax.rsqrt(var + EPS)
    pick = first_half((width // 2, LANES))
    w = w_ref[...]
    for at in range(rows_dev // 2):
        even, odd = parts[:, 2 * at, :], parts[:, 2 * at + 1, :]
        normed = jnp.concatenate(
            [jnp.where(pick, even, swap(odd)), jnp.where(pick, swap(even), odd)], axis=0
        ).astype(jnp.bfloat16)
        mixed = dot_t(normed, w, (0, 0))
        update = gate_ref[at * LANES : (at + 1) * LANES, :] * mixed
        out_ref[2 * at : 2 * at + 2] = update.astype(jnp.bfloat16).reshape(2, cols_dev, width)


def vmem():
    return pl.BlockSpec(memory_space=pltpu.VMEM)


def tiled(n_rows, n_chan, pair, block_mask, w_in, w_out):
    rows_dev, cols_dev, width = pair.shape
    n_dev = n_rows * n_chan
    groups = width // (2 * n_dev)
    slab = groups * SUBLANES
    sent, gate = pl.pallas_call(
        project_kernel,
        out_shape=(
            jax.ShapeDtypeStruct((n_dev, 2 * slab, LANES), jnp.bfloat16),
            jax.ShapeDtypeStruct((rows_dev * cols_dev, width), jnp.float32),
        ),
        in_specs=[pl.BlockSpec(memory_space=pltpu.SMEM), vmem(), vmem()],
        out_specs=(vmem(), vmem()),
        scratch_shapes=[pltpu.VMEM((2, width // 2, SUBLANES, LANES), jnp.float32)],
        name="project",
    )(block_mask, pair, w_in)
    got = lax.all_to_all(sent, AXES, split_axis=0, concat_axis=0, tiled=True)
    prod = pl.pallas_call(
        product_kernel,
        out_shape=jax.ShapeDtypeStruct((n_rows, n_chan, slab, LANES), jnp.bfloat16),
        in_specs=[vmem()],
        out_specs=vmem(),
        name="product",
    )(got.reshape(n_rows, n_chan, 2 * slab, LANES))
    back = lax.all_to_all(
        prod.reshape(n_dev, slab, LANES), AXES, split_axis=0, concat_axis=0, tiled=True
    )
    return pl.pallas_call(
        finish_kernel,
        out_shape=jax.ShapeDtypeStruct(pair.shape, jnp.bfloat16),
        in_specs=[vmem()] * 3,
        out_specs=vmem(),
        scratch_shapes=[pltpu.VMEM((width // 2, SUBLANES, LANES), jnp.float32)],
        name="finish",
    )(back, gate, w_out)


def solution(mesh):
    n_rows, n_chan = mesh.shape["rows"], mesh.shape["chan"]

    def on_device(pair, block_mask, w_in, w_out):
        rows_dev, cols_dev, width = pair.shape
        fits = (
            n_chan == 2
            and rows_dev == SUBLANES
            and 2 * cols_dev == LANES
            and width == LANES
            and width % (4 * n_rows * n_chan) == 0
        )
        if fits:
            return tiled(n_rows, n_chan, pair, block_mask, w_in, w_out)
        return gathered(pair, block_mask, w_in, w_out)

    placed = (P("rows", "chan", None), P(), P(), P())
    return jax.shard_map(
        on_device, mesh=mesh, in_specs=placed, out_specs=P("rows", "chan", None), check_vma=False
    )
```

```python
import jax
import jax.numpy as jnp
from jax import lax
from jax.experimental import pallas as pl
from jax.experimental.pallas import tpu as pltpu
from jax.sharding import PartitionSpec as P

BLOCK = 128
LANES = 128
SUBLANES = 8
EPS = 1e-05
AXES = ("rows", "chan")
GRANT = pltpu.CompilerParams(vmem_limit_bytes=4 * 1024 * 1024)


def layer_norm(values):
    mean = jnp.mean(values, axis=-1, keepdims=True)
    centered = values - mean
    var = jnp.mean(centered * centered, axis=-1, keepdims=True)
    return centered / jnp.sqrt(var + EPS)


def channel_product(left, piece):
    return jnp.einsum("cik,cjk->cij", left, piece, preferred_element_type=jnp.float32)


def gathered(pair, block_mask, w_in, w_out):
    rows_dev, cols_dev, width = pair.shape
    n_blocks = block_mask.shape[0]
    row_start = lax.axis_index("rows") * rows_dev
    col_start = lax.axis_index("chan") * cols_dev
    row_ids = row_start + lax.broadcasted_iota(jnp.int32, (rows_dev, n_blocks), 0)
    col_ids = col_start + lax.broadcasted_iota(jnp.int32, (cols_dev, n_blocks), 0)
    rows_hot = (
        row_ids // BLOCK == lax.broadcasted_iota(jnp.int32, (rows_dev, n_blocks), 1)
    ).astype(jnp.float32)
    cols_hot = (
        col_ids // BLOCK == lax.broadcasted_iota(jnp.int32, (cols_dev, n_blocks), 1)
    ).astype(jnp.float32)
    mask_float = block_mask.astype(jnp.float32)
    local_mask = jnp.dot(jnp.dot(rows_hot, mask_float), cols_hot.T)[:, :, None]
    normed = layer_norm(pair.astype(jnp.float32)).astype(jnp.bfloat16)
    proj = jnp.dot(normed.reshape(-1, width), w_in, preferred_element_type=jnp.float32).reshape(
        rows_dev, cols_dev, 5 * width
    )
    left = (jax.nn.sigmoid(proj[..., :width]) * proj[..., width : 2 * width] * local_mask).astype(
        jnp.bfloat16
    )
    right = (
        jax.nn.sigmoid(proj[..., 2 * width : 3 * width])
        * proj[..., 3 * width : 4 * width]
        * local_mask
    ).astype(jnp.bfloat16)
    gate = jax.nn.sigmoid(proj[..., 4 * width :])
    left_t = jnp.transpose(left, (2, 0, 1))
    right_t = jnp.transpose(right, (2, 0, 1))
    left_ch, right_ch = (
        lax.all_to_all(left_t, "chan", split_axis=0, concat_axis=2, tiled=True),
        lax.all_to_all(right_t, "chan", split_axis=0, concat_axis=2, tiled=True),
    )
    prod_ch = channel_product(left_ch, lax.all_gather(right_ch, "rows", axis=1, tiled=True))
    prod_back = lax.all_to_all(prod_ch, "chan", split_axis=2, concat_axis=0, tiled=True)
    prod = jnp.transpose(prod_back, (1, 2, 0))
    normed_prod = layer_norm(prod).astype(jnp.bfloat16)
    mixed = jnp.dot(
        normed_prod.reshape(-1, width), w_out, preferred_element_type=jnp.float32
    ).reshape(rows_dev, cols_dev, width)
    return (gate * mixed).astype(jnp.bfloat16)


def dot_t(a, b, contract):
    return lax.dot_general(a, b, ((contract[:1], contract[1:]), ((), ())), preferred_element_type=jnp.float32)


def first_half(shape):
    return lax.broadcasted_iota(jnp.int32, shape, len(shape) - 1) < LANES // 2


def swap(values):
    return pltpu.roll(values, LANES // 2, values.ndim - 1)


def project_kernel(mask_ref, pair_hbm, w_hbm, out_ref, gate_ref, pair_ref, w_ref, parts, sems):
    copies = [
        pltpu.make_async_copy(src, dst, sems.at[at])
        for at, (src, dst) in enumerate(((pair_hbm, pair_ref), (w_hbm, w_ref)))
    ]
    for copy in copies:
        copy.start()
    rows_dev, cols_dev, width = pair_ref.shape
    tokens, half = rows_dev * cols_dev, width // 2
    row_block = lax.axis_index("rows") * rows_dev // BLOCK
    col_block = lax.axis_index("chan") * cols_dev // BLOCK

    across = (width, width)
    diagonal = lax.broadcasted_iota(jnp.int32, across, 0) == lax.broadcasted_iota(jnp.int32, across, 1)
    less_mean = jnp.where(diagonal, 1.0 - 1.0 / width, -1.0 / width).astype(jnp.bfloat16)
    copies[0].wait()
    centered = dot_t(less_mean, pair_ref[...].reshape(tokens, width), (1, 1))
    var = jnp.sum(centered * centered, axis=0, keepdims=True) * (1.0 / width)
    normed = (centered * lax.rsqrt(var + EPS)).astype(jnp.bfloat16)

    copies[1].wait()
    half_mask = 0.5 * mask_ref[row_block, col_block].astype(jnp.float32)
    pick = first_half((half, LANES))
    n_dev, slab = out_ref.shape[0], out_ref.shape[1] // 2
    for side in range(2):
        begin = 2 * side * width
        gates = dot_t(w_ref[:, begin : begin + width], normed, (0, 0))
        values = dot_t(w_ref[:, begin + width : begin + 2 * width], normed, (0, 0))
        held = (jnp.tanh(0.5 * gates) * half_mask + half_mask) * values
        for at in range(tokens // LANES):
            low_c = held[:half, at * LANES : (at + 1) * LANES]
            high_c = held[half:, at * LANES : (at + 1) * LANES]
            parts[side, :, 2 * at, :] = jnp.where(pick, low_c, swap(high_c))
            parts[side, :, 2 * at + 1, :] = jnp.where(pick, swap(low_c), high_c)
        out_ref[:, side * slab : (side + 1) * slab, :] = (
            parts[side].reshape(n_dev, slab, LANES).astype(jnp.bfloat16)
        )
    gate = dot_t(w_ref[:, 4 * width :], normed, (0, 0))
    gate_ref[...] = 0.5 * jnp.tanh(0.5 * gate) + 0.5


def product_kernel(in_ref, out_ref):
    n_rows, n_chan, slabs, _ = in_ref.shape
    slab = slabs // 2
    groups = slab // SUBLANES
    tokens = n_rows * SUBLANES

    def side(at):
        values = in_ref[:, :, at * slab : (at + 1) * slab, :].astype(jnp.float32)
        return values.reshape(n_rows, n_chan, groups, SUBLANES, LANES)

    left, right = side(0), side(1)
    pick = first_half((tokens, LANES))
    made = []
    for g in range(groups):
        a = [left[:, x, g].reshape(tokens, LANES) for x in range(n_chan)]
        b = [right[:, x, g].reshape(tokens, LANES) for x in range(n_chan)]
        rows = [
            jnp.concatenate([jnp.where(pick, v, 0.0) for v in a], axis=1),
            jnp.concatenate([jnp.where(pick, 0.0, v) for v in a], axis=1),
        ]
        a = jnp.concatenate(rows, axis=0).astype(jnp.bfloat16)
        b = jnp.concatenate(b, axis=1).astype(jnp.bfloat16)
        prod = dot_t(a, b, (1, 1))
        made.append((prod[:tokens], prod[tokens:]))
    blocks = [
        [jnp.where(pick, low, swap(high)) for low, high in made],
        [jnp.where(pick, swap(low), high) for low, high in made],
    ]
    for x in range(n_chan):
        block = jnp.concatenate([v.reshape(n_rows, SUBLANES, LANES) for v in blocks[x]], axis=1)
        out_ref[:, x] = block.astype(jnp.bfloat16)


def finish_kernel(prod_ref, gate_ref, w_ref, out_ref, parts):
    n_dev, slab, _ = prod_ref.shape
    rows_dev, cols_dev, width = out_ref.shape
    prod = prod_ref[...].astype(jnp.float32).reshape(n_dev * slab // SUBLANES, SUBLANES, LANES)
    total = jnp.sum(prod, axis=0)
    mean = (total + swap(total)) * (1.0 / width)
    centered = prod - mean
    total = jnp.sum(centered * centered, axis=0)
    var = (total + swap(total)) * (1.0 / width)
    parts[...] = centered * lax.rsqrt(var + EPS)
    pick = first_half((width // 2, LANES))
    w = w_ref[...]
    for at in range(rows_dev // 2):
        even, odd = parts[:, 2 * at, :], parts[:, 2 * at + 1, :]
        normed = jnp.concatenate(
            [jnp.where(pick, even, swap(odd)), jnp.where(pick, swap(even), odd)], axis=0
        ).astype(jnp.bfloat16)
        update = gate_ref[:, at * LANES : (at + 1) * LANES] * dot_t(w, normed, (0, 0))
        out_ref[2 * at : 2 * at + 2] = update.astype(jnp.bfloat16).T.reshape(2, cols_dev, width)


def vmem():
    return pl.BlockSpec(memory_space=pltpu.VMEM)


def tiled(n_rows, n_chan, pair, block_mask, w_in, w_out):
    rows_dev, cols_dev, width = pair.shape
    n_dev = n_rows * n_chan
    groups = width // (2 * n_dev)
    slab = groups * SUBLANES
    sent, gate = pl.pallas_call(
        project_kernel,
        out_shape=(
            jax.ShapeDtypeStruct((n_dev, 2 * slab, LANES), jnp.bfloat16),
            jax.ShapeDtypeStruct((width, rows_dev * cols_dev), jnp.float32),
        ),
        in_specs=[pl.BlockSpec(memory_space=pltpu.SMEM)] + [pl.BlockSpec(memory_space=pltpu.HBM)] * 2,
        out_specs=(vmem(), vmem()),
        scratch_shapes=[
            pltpu.VMEM(pair.shape, pair.dtype),
            pltpu.VMEM(w_in.shape, w_in.dtype),
            pltpu.VMEM((2, width // 2, SUBLANES, LANES), jnp.float32),
            pltpu.SemaphoreType.DMA((2,)),
        ],
        compiler_params=GRANT,
        name="project",
    )(block_mask, *(pltpu.with_memory_space_constraint(v, pltpu.HBM) for v in (pair, w_in)))
    got = lax.all_to_all(sent, AXES, split_axis=0, concat_axis=0, tiled=True)
    prod = pl.pallas_call(
        product_kernel,
        out_shape=jax.ShapeDtypeStruct((n_rows, n_chan, slab, LANES), jnp.bfloat16),
        in_specs=[vmem()],
        out_specs=vmem(),
        compiler_params=GRANT,
        name="product",
    )(got.reshape(n_rows, n_chan, 2 * slab, LANES))
    back = lax.all_to_all(
        prod.reshape(n_dev, slab, LANES), AXES, split_axis=0, concat_axis=0, tiled=True
    )
    return pl.pallas_call(
        finish_kernel,
        out_shape=jax.ShapeDtypeStruct(pair.shape, jnp.bfloat16),
        in_specs=[vmem()] * 3,
        out_specs=vmem(),
        scratch_shapes=[pltpu.VMEM((width // 2, SUBLANES, LANES), jnp.float32)],
        compiler_params=GRANT,
        name="finish",
    )(back, gate, w_out)


def solution(mesh):
    n_rows, n_chan = mesh.shape["rows"], mesh.shape["chan"]

    def on_device(pair, block_mask, w_in, w_out):
        rows_dev, cols_dev, width = pair.shape
        fits = (
            n_chan == 2
            and rows_dev == SUBLANES
            and 2 * cols_dev == LANES
            and width == LANES
            and width % (4 * n_rows * n_chan) == 0
        )
        if fits:
            return tiled(n_rows, n_chan, pair, block_mask, w_in, w_out)
        return gathered(pair, block_mask, w_in, w_out)

    placed = (P("rows", "chan", None), P(), P(), P())
    return jax.shard_map(
        on_device, mesh=mesh, in_specs=placed, out_specs=P("rows", "chan", None), check_vma=False
    )
```

```python
import functools

import jax
import jax.numpy as jnp
from jax import lax
from jax.experimental import pallas as pl
from jax.experimental.pallas import tpu as pltpu
from jax.sharding import PartitionSpec as P

BLOCK = 128
LANES = 128
SUBLANES = 8
EPS = 1e-05
AXES = ("rows", "chan")
GRANT = pltpu.CompilerParams(vmem_limit_bytes=4 * 1024 * 1024)


def layer_norm(values):
    mean = jnp.mean(values, axis=-1, keepdims=True)
    centered = values - mean
    var = jnp.mean(centered * centered, axis=-1, keepdims=True)
    return centered / jnp.sqrt(var + EPS)


def channel_product(left, piece):
    return jnp.einsum("cik,cjk->cij", left, piece, preferred_element_type=jnp.float32)


def gathered(pair, block_mask, w_in, w_out):
    rows_dev, cols_dev, width = pair.shape
    n_blocks = block_mask.shape[0]
    row_start = lax.axis_index("rows") * rows_dev
    col_start = lax.axis_index("chan") * cols_dev
    row_ids = row_start + lax.broadcasted_iota(jnp.int32, (rows_dev, n_blocks), 0)
    col_ids = col_start + lax.broadcasted_iota(jnp.int32, (cols_dev, n_blocks), 0)
    rows_hot = (
        row_ids // BLOCK == lax.broadcasted_iota(jnp.int32, (rows_dev, n_blocks), 1)
    ).astype(jnp.float32)
    cols_hot = (
        col_ids // BLOCK == lax.broadcasted_iota(jnp.int32, (cols_dev, n_blocks), 1)
    ).astype(jnp.float32)
    mask_float = block_mask.astype(jnp.float32)
    local_mask = jnp.dot(jnp.dot(rows_hot, mask_float), cols_hot.T)[:, :, None]
    normed = layer_norm(pair.astype(jnp.float32)).astype(jnp.bfloat16)
    proj = jnp.dot(normed.reshape(-1, width), w_in, preferred_element_type=jnp.float32).reshape(
        rows_dev, cols_dev, 5 * width
    )
    left = (jax.nn.sigmoid(proj[..., :width]) * proj[..., width : 2 * width] * local_mask).astype(
        jnp.bfloat16
    )
    right = (
        jax.nn.sigmoid(proj[..., 2 * width : 3 * width])
        * proj[..., 3 * width : 4 * width]
        * local_mask
    ).astype(jnp.bfloat16)
    gate = jax.nn.sigmoid(proj[..., 4 * width :])
    left_t = jnp.transpose(left, (2, 0, 1))
    right_t = jnp.transpose(right, (2, 0, 1))
    left_ch, right_ch = (
        lax.all_to_all(left_t, "chan", split_axis=0, concat_axis=2, tiled=True),
        lax.all_to_all(right_t, "chan", split_axis=0, concat_axis=2, tiled=True),
    )
    prod_ch = channel_product(left_ch, lax.all_gather(right_ch, "rows", axis=1, tiled=True))
    prod_back = lax.all_to_all(prod_ch, "chan", split_axis=2, concat_axis=0, tiled=True)
    prod = jnp.transpose(prod_back, (1, 2, 0))
    normed_prod = layer_norm(prod).astype(jnp.bfloat16)
    mixed = jnp.dot(
        normed_prod.reshape(-1, width), w_out, preferred_element_type=jnp.float32
    ).reshape(rows_dev, cols_dev, width)
    return (gate * mixed).astype(jnp.bfloat16)


def dot_t(a, b, contract):
    return lax.dot_general(a, b, ((contract[:1], contract[1:]), ((), ())), preferred_element_type=jnp.float32)


def first_half(shape):
    return lax.broadcasted_iota(jnp.int32, shape, len(shape) - 1) < LANES // 2


def swap(values):
    return pltpu.roll(values, LANES // 2, values.ndim - 1)


def project_kernel(mask_ref, pair_hbm, w_hbm, out_ref, gate_ref, pair_ref, w_ref, parts, sems):
    copies = [
        pltpu.make_async_copy(src, dst, sems.at[at])
        for at, (src, dst) in enumerate(((pair_hbm, pair_ref), (w_hbm, w_ref)))
    ]
    for copy in copies:
        copy.start()
    rows_dev, cols_dev, width = pair_ref.shape
    tokens, half = rows_dev * cols_dev, width // 2
    row_block = lax.axis_index("rows") * rows_dev // BLOCK
    col_block = lax.axis_index("chan") * cols_dev // BLOCK

    across = (width, width)
    diagonal = lax.broadcasted_iota(jnp.int32, across, 0) == lax.broadcasted_iota(jnp.int32, across, 1)
    less_mean = jnp.where(diagonal, 1.0 - 1.0 / width, -1.0 / width).astype(jnp.bfloat16)
    copies[0].wait()
    centered = dot_t(less_mean, pair_ref[...].reshape(tokens, width), (1, 1))
    var = jnp.sum(centered * centered, axis=0, keepdims=True) * (1.0 / width)
    normed = (centered * lax.rsqrt(var + EPS)).astype(jnp.bfloat16)

    copies[1].wait()
    half_mask = 0.5 * mask_ref[row_block, col_block].astype(jnp.float32)
    pick = first_half((half, LANES))
    n_dev, slab = out_ref.shape[0], out_ref.shape[1] // 2
    for side in range(2):
        begin = 2 * side * width
        gates = dot_t(w_ref[:, begin : begin + width], normed, (0, 0))
        values = dot_t(w_ref[:, begin + width : begin + 2 * width], normed, (0, 0))
        held = (jnp.tanh(0.5 * gates) * half_mask + half_mask) * values
        for at in range(tokens // LANES):
            low_c = held[:half, at * LANES : (at + 1) * LANES]
            high_c = held[half:, at * LANES : (at + 1) * LANES]
            parts[side, :, 2 * at, :] = jnp.where(pick, low_c, swap(high_c))
            parts[side, :, 2 * at + 1, :] = jnp.where(pick, swap(low_c), high_c)
        out_ref[:, side * slab : (side + 1) * slab, :] = (
            parts[side].reshape(n_dev, slab, LANES).astype(jnp.bfloat16)
        )
    gate = dot_t(w_ref[:, 4 * width :], normed, (0, 0))
    gate_ref[...] = 0.5 * jnp.tanh(0.5 * gate) + 0.5


def product_kernel(n_rows, n_chan, spots, in_ref, out_ref):
    slab = out_ref.shape[1]
    groups = slab // SUBLANES
    tokens = n_rows * SUBLANES

    def side(at):
        values = in_ref[:, at * slab : (at + 1) * slab, :].astype(jnp.float32)
        values = jnp.stack([values[spot] for spot in spots])
        return values.reshape(n_rows, n_chan, groups, SUBLANES, LANES)

    left, right = side(0), side(1)
    pick = first_half((tokens, LANES))
    made = []
    for g in range(groups):
        a = [left[:, x, g].reshape(tokens, LANES) for x in range(n_chan)]
        b = [right[:, x, g].reshape(tokens, LANES) for x in range(n_chan)]
        rows = [
            jnp.concatenate([jnp.where(pick, v, 0.0) for v in a], axis=1),
            jnp.concatenate([jnp.where(pick, 0.0, v) for v in a], axis=1),
        ]
        a = jnp.concatenate(rows, axis=0).astype(jnp.bfloat16)
        b = jnp.concatenate(b, axis=1).astype(jnp.bfloat16)
        prod = dot_t(a, b, (1, 1))
        made.append((prod[:tokens], prod[tokens:]))
    blocks = [
        [jnp.where(pick, low, swap(high)) for low, high in made],
        [jnp.where(pick, swap(low), high) for low, high in made],
    ]
    for x in range(n_chan):
        block = jnp.concatenate([v.reshape(n_rows, SUBLANES, LANES) for v in blocks[x]], axis=1)
        block = block.astype(jnp.bfloat16)
        for row in range(n_rows):
            out_ref[spots[row * n_chan + x]] = block[row]


def finish_kernel(prod_ref, gate_ref, w_ref, out_ref, parts):
    n_dev, slab, _ = prod_ref.shape
    rows_dev, cols_dev, width = out_ref.shape
    prod = prod_ref[...].astype(jnp.float32).reshape(n_dev * slab // SUBLANES, SUBLANES, LANES)
    total = jnp.sum(prod, axis=0)
    mean = (total + swap(total)) * (1.0 / width)
    centered = prod - mean
    total = jnp.sum(centered * centered, axis=0)
    var = (total + swap(total)) * (1.0 / width)
    parts[...] = centered * lax.rsqrt(var + EPS)
    pick = first_half((width // 2, LANES))
    w = w_ref[...]
    for at in range(rows_dev // 2):
        even, odd = parts[:, 2 * at, :], parts[:, 2 * at + 1, :]
        normed = jnp.concatenate(
            [jnp.where(pick, even, swap(odd)), jnp.where(pick, swap(even), odd)], axis=0
        ).astype(jnp.bfloat16)
        update = gate_ref[:, at * LANES : (at + 1) * LANES] * dot_t(w, normed, (0, 0))
        out_ref[2 * at : 2 * at + 2] = update.astype(jnp.bfloat16).T.reshape(2, cols_dev, width)


def vmem():
    return pl.BlockSpec(memory_space=pltpu.VMEM)


def exchange_order(n_dev):
    stride = n_dev // 8 * 2 + 1
    return [place * stride % n_dev for place in range(n_dev)]


def exchange(values, order):
    return lax.all_to_all(
        values, AXES, split_axis=0, concat_axis=0, axis_index_groups=[order], tiled=True
    )


def tiled(n_rows, n_chan, pair, block_mask, w_in, w_out):
    rows_dev, cols_dev, width = pair.shape
    n_dev = n_rows * n_chan
    groups = width // (2 * n_dev)
    slab = groups * SUBLANES
    order = exchange_order(n_dev)
    spots = [order.index(device) for device in range(n_dev)]
    sent, gate = pl.pallas_call(
        project_kernel,
        out_shape=(
            jax.ShapeDtypeStruct((n_dev, 2 * slab, LANES), jnp.bfloat16),
            jax.ShapeDtypeStruct((width, rows_dev * cols_dev), jnp.float32),
        ),
        in_specs=[pl.BlockSpec(memory_space=pltpu.SMEM)] + [pl.BlockSpec(memory_space=pltpu.HBM)] * 2,
        out_specs=(vmem(), vmem()),
        scratch_shapes=[
            pltpu.VMEM(pair.shape, pair.dtype),
            pltpu.VMEM(w_in.shape, w_in.dtype),
            pltpu.VMEM((2, width // 2, SUBLANES, LANES), jnp.float32),
            pltpu.SemaphoreType.DMA((2,)),
        ],
        compiler_params=GRANT,
        name="project",
    )(block_mask, *(pltpu.with_memory_space_constraint(v, pltpu.HBM) for v in (pair, w_in)))
    got = exchange(sent, order)
    prod = pl.pallas_call(
        functools.partial(product_kernel, n_rows, n_chan, spots),
        out_shape=jax.ShapeDtypeStruct((n_dev, slab, LANES), jnp.bfloat16),
        in_specs=[vmem()],
        out_specs=vmem(),
        compiler_params=GRANT,
        name="product",
    )(got)
    back = exchange(prod, order)
    return pl.pallas_call(
        finish_kernel,
        out_shape=jax.ShapeDtypeStruct(pair.shape, jnp.bfloat16),
        in_specs=[vmem()] * 3,
        out_specs=vmem(),
        scratch_shapes=[pltpu.VMEM((width // 2, SUBLANES, LANES), jnp.float32)],
        compiler_params=GRANT,
        name="finish",
    )(back, gate, w_out)


def solution(mesh):
    n_rows, n_chan = mesh.shape["rows"], mesh.shape["chan"]

    def on_device(pair, block_mask, w_in, w_out):
        rows_dev, cols_dev, width = pair.shape
        fits = (
            n_chan == 2
            and rows_dev == SUBLANES
            and 2 * cols_dev == LANES
            and width == LANES
            and width % (4 * n_rows * n_chan) == 0
        )
        if fits:
            return tiled(n_rows, n_chan, pair, block_mask, w_in, w_out)
        return gathered(pair, block_mask, w_in, w_out)

    placed = (P("rows", "chan", None), P(), P(), P())
    return jax.shard_map(
        on_device, mesh=mesh, in_specs=placed, out_specs=P("rows", "chan", None), check_vma=False
    )
```

```python
import functools

import jax
import jax.numpy as jnp
from jax import lax
from jax.experimental import pallas as pl
from jax.experimental.pallas import tpu as pltpu
from jax.sharding import PartitionSpec as P

BLOCK = 128
LANES = 128
SUBLANES = 8
EPS = 1e-05
AXES = ("rows", "chan")
GRANT = pltpu.CompilerParams(vmem_limit_bytes=4 * 1024 * 1024)


def layer_norm(values):
    mean = jnp.mean(values, axis=-1, keepdims=True)
    centered = values - mean
    var = jnp.mean(centered * centered, axis=-1, keepdims=True)
    return centered / jnp.sqrt(var + EPS)


def channel_product(left, piece):
    return jnp.einsum("cik,cjk->cij", left, piece, preferred_element_type=jnp.float32)


def gathered(pair, block_mask, w_in, w_out):
    rows_dev, cols_dev, width = pair.shape
    n_blocks = block_mask.shape[0]
    row_start = lax.axis_index("rows") * rows_dev
    col_start = lax.axis_index("chan") * cols_dev
    row_ids = row_start + lax.broadcasted_iota(jnp.int32, (rows_dev, n_blocks), 0)
    col_ids = col_start + lax.broadcasted_iota(jnp.int32, (cols_dev, n_blocks), 0)
    rows_hot = (
        row_ids // BLOCK == lax.broadcasted_iota(jnp.int32, (rows_dev, n_blocks), 1)
    ).astype(jnp.float32)
    cols_hot = (
        col_ids // BLOCK == lax.broadcasted_iota(jnp.int32, (cols_dev, n_blocks), 1)
    ).astype(jnp.float32)
    mask_float = block_mask.astype(jnp.float32)
    local_mask = jnp.dot(jnp.dot(rows_hot, mask_float), cols_hot.T)[:, :, None]
    normed = layer_norm(pair.astype(jnp.float32)).astype(jnp.bfloat16)
    proj = jnp.dot(normed.reshape(-1, width), w_in, preferred_element_type=jnp.float32).reshape(
        rows_dev, cols_dev, 5 * width
    )
    left = (jax.nn.sigmoid(proj[..., :width]) * proj[..., width : 2 * width] * local_mask).astype(
        jnp.bfloat16
    )
    right = (
        jax.nn.sigmoid(proj[..., 2 * width : 3 * width])
        * proj[..., 3 * width : 4 * width]
        * local_mask
    ).astype(jnp.bfloat16)
    gate = jax.nn.sigmoid(proj[..., 4 * width :])
    left_t = jnp.transpose(left, (2, 0, 1))
    right_t = jnp.transpose(right, (2, 0, 1))
    left_ch, right_ch = (
        lax.all_to_all(left_t, "chan", split_axis=0, concat_axis=2, tiled=True),
        lax.all_to_all(right_t, "chan", split_axis=0, concat_axis=2, tiled=True),
    )
    prod_ch = channel_product(left_ch, lax.all_gather(right_ch, "rows", axis=1, tiled=True))
    prod_back = lax.all_to_all(prod_ch, "chan", split_axis=2, concat_axis=0, tiled=True)
    prod = jnp.transpose(prod_back, (1, 2, 0))
    normed_prod = layer_norm(prod).astype(jnp.bfloat16)
    mixed = jnp.dot(
        normed_prod.reshape(-1, width), w_out, preferred_element_type=jnp.float32
    ).reshape(rows_dev, cols_dev, width)
    return (gate * mixed).astype(jnp.bfloat16)


def dot_t(a, b, contract):
    return lax.dot_general(a, b, ((contract[:1], contract[1:]), ((), ())), preferred_element_type=jnp.float32)


def first_half(shape):
    return lax.broadcasted_iota(jnp.int32, shape, len(shape) - 1) < LANES // 2


def swap(values):
    return pltpu.roll(values, LANES // 2, values.ndim - 1)


def project_kernel(owned, mask_ref, pair_hbm, w_hbm, out_ref, gate_ref, pair_ref, w_ref, parts, sems):
    copies = [
        pltpu.make_async_copy(src, dst, sems.at[at])
        for at, (src, dst) in enumerate(((pair_hbm, pair_ref), (w_hbm, w_ref)))
    ]
    for copy in copies:
        copy.start()
    rows_dev, cols_dev, width = pair_ref.shape
    tokens, half = rows_dev * cols_dev, width // 2
    row_block = lax.axis_index("rows") * rows_dev // BLOCK
    col_block = lax.axis_index("chan") * cols_dev // BLOCK

    across = (width, width)
    diagonal = lax.broadcasted_iota(jnp.int32, across, 0) == lax.broadcasted_iota(jnp.int32, across, 1)
    less_mean = jnp.where(diagonal, 1.0 - 1.0 / width, -1.0 / width).astype(jnp.bfloat16)
    copies[0].wait()
    centered = dot_t(less_mean, pair_ref[...].reshape(tokens, width), (1, 1))
    var = jnp.sum(centered * centered, axis=0, keepdims=True) * (1.0 / width)
    normed = (centered * lax.rsqrt(var + EPS)).astype(jnp.bfloat16)

    copies[1].wait()
    half_mask = 0.5 * mask_ref[row_block, col_block].astype(jnp.float32)
    pick = first_half((half, LANES))
    n_dev, slab = out_ref.shape[0], out_ref.shape[1] // 2
    for side in range(2):
        begin = 2 * side * width
        gates = dot_t(w_ref[:, begin : begin + width], normed, (0, 0))
        values = dot_t(w_ref[:, begin + width : begin + 2 * width], normed, (0, 0))
        held = (jnp.tanh(0.5 * gates) * half_mask + half_mask) * values
        for at in range(tokens // LANES):
            low_c = held[:half, at * LANES : (at + 1) * LANES]
            high_c = held[half:, at * LANES : (at + 1) * LANES]
            parts[side, :, 2 * at, :] = jnp.where(pick, low_c, swap(high_c))
            parts[side, :, 2 * at + 1, :] = jnp.where(pick, swap(low_c), high_c)
        block = parts[side].reshape(n_dev, slab, LANES).astype(jnp.bfloat16)
        for place, group in enumerate(owned):
            out_ref[place, side * slab : (side + 1) * slab, :] = block[group]
    gate = dot_t(w_ref[:, 4 * width :], normed, (0, 0))
    gate_ref[...] = 0.5 * jnp.tanh(0.5 * gate) + 0.5


def product_kernel(n_rows, n_chan, spots, in_ref, out_ref):
    slab = out_ref.shape[1]
    groups = slab // SUBLANES
    tokens = n_rows * SUBLANES

    def side(at):
        values = in_ref[:, at * slab : (at + 1) * slab, :].astype(jnp.float32)
        values = jnp.stack([values[spot] for spot in spots[0]])
        return values.reshape(n_rows, n_chan, groups, SUBLANES, LANES)

    left, right = side(0), side(1)
    pick = first_half((tokens, LANES))
    made = []
    for g in range(groups):
        a = [left[:, x, g].reshape(tokens, LANES) for x in range(n_chan)]
        b = [right[:, x, g].reshape(tokens, LANES) for x in range(n_chan)]
        rows = [
            jnp.concatenate([jnp.where(pick, v, 0.0) for v in a], axis=1),
            jnp.concatenate([jnp.where(pick, 0.0, v) for v in a], axis=1),
        ]
        a = jnp.concatenate(rows, axis=0).astype(jnp.bfloat16)
        b = jnp.concatenate(b, axis=1).astype(jnp.bfloat16)
        prod = dot_t(a, b, (1, 1))
        made.append((prod[:tokens], prod[tokens:]))
    blocks = [
        [jnp.where(pick, low, swap(high)) for low, high in made],
        [jnp.where(pick, swap(low), high) for low, high in made],
    ]
    for x in range(n_chan):
        block = jnp.concatenate([v.reshape(n_rows, SUBLANES, LANES) for v in blocks[x]], axis=1)
        block = block.astype(jnp.bfloat16)
        for row in range(n_rows):
            out_ref[spots[1][row * n_chan + x]] = block[row]


def finish_kernel(prod_ref, gate_ref, w_ref, out_ref, parts):
    n_dev, slab, _ = prod_ref.shape
    rows_dev, cols_dev, width = out_ref.shape
    prod = prod_ref[...].astype(jnp.float32).reshape(n_dev * slab // SUBLANES, SUBLANES, LANES)
    total = jnp.sum(prod, axis=0)
    mean = (total + swap(total)) * (1.0 / width)
    centered = prod - mean
    total = jnp.sum(centered * centered, axis=0)
    var = (total + swap(total)) * (1.0 / width)
    parts[...] = centered * lax.rsqrt(var + EPS)
    pick = first_half((width // 2, LANES))
    w = w_ref[...]
    for at in range(rows_dev // 2):
        even, odd = parts[:, 2 * at, :], parts[:, 2 * at + 1, :]
        normed = jnp.concatenate(
            [jnp.where(pick, even, swap(odd)), jnp.where(pick, swap(even), odd)], axis=0
        ).astype(jnp.bfloat16)
        update = gate_ref[:, at * LANES : (at + 1) * LANES] * dot_t(w, normed, (0, 0))
        out_ref[2 * at : 2 * at + 2] = update.astype(jnp.bfloat16).T.reshape(2, cols_dev, width)


def vmem():
    return pl.BlockSpec(memory_space=pltpu.VMEM)


def orders(n_rows, n_chan):
    n_dev = n_rows * n_chan
    quarter = max(n_rows // 4, 1)
    there = [
        (row + at) * n_chan + x
        for x in range(n_chan)
        for at in range(quarter)
        for row in range(n_rows - quarter, -1, -quarter)
    ]
    stride = n_dev // 8 * 2 + 1
    back = [place * stride % n_dev for place in range(n_dev)]
    return there, back


def exchange(values, order):
    return lax.all_to_all(
        values, AXES, split_axis=0, concat_axis=0, axis_index_groups=[order], tiled=True
    )


def tiled(n_rows, n_chan, pair, block_mask, w_in, w_out):
    rows_dev, cols_dev, width = pair.shape
    n_dev = n_rows * n_chan
    groups = width // (2 * n_dev)
    slab = groups * SUBLANES
    there, back = orders(n_rows, n_chan)
    owned = [back.index(device) for device in there]
    spots = [[order.index(device) for device in range(n_dev)] for order in (there, back)]
    sent, gate = pl.pallas_call(
        functools.partial(project_kernel, owned),
        out_shape=(
            jax.ShapeDtypeStruct((n_dev, 2 * slab, LANES), jnp.bfloat16),
            jax.ShapeDtypeStruct((width, rows_dev * cols_dev), jnp.float32),
        ),
        in_specs=[pl.BlockSpec(memory_space=pltpu.SMEM)] + [pl.BlockSpec(memory_space=pltpu.HBM)] * 2,
        out_specs=(vmem(), vmem()),
        scratch_shapes=[
            pltpu.VMEM(pair.shape, pair.dtype),
            pltpu.VMEM(w_in.shape, w_in.dtype),
            pltpu.VMEM((2, width // 2, SUBLANES, LANES), jnp.float32),
            pltpu.SemaphoreType.DMA((2,)),
        ],
        compiler_params=GRANT,
        name="project",
    )(block_mask, *(pltpu.with_memory_space_constraint(v, pltpu.HBM) for v in (pair, w_in)))
    got = exchange(sent, there)
    prod = pl.pallas_call(
        functools.partial(product_kernel, n_rows, n_chan, spots),
        out_shape=jax.ShapeDtypeStruct((n_dev, slab, LANES), jnp.bfloat16),
        in_specs=[vmem()],
        out_specs=vmem(),
        compiler_params=GRANT,
        name="product",
    )(got)
    returned = exchange(prod, back)
    return pl.pallas_call(
        finish_kernel,
        out_shape=jax.ShapeDtypeStruct(pair.shape, jnp.bfloat16),
        in_specs=[vmem()] * 3,
        out_specs=vmem(),
        scratch_shapes=[pltpu.VMEM((width // 2, SUBLANES, LANES), jnp.float32)],
        compiler_params=GRANT,
        name="finish",
    )(returned, gate, w_out)


def solution(mesh):
    n_rows, n_chan = mesh.shape["rows"], mesh.shape["chan"]

    def on_device(pair, block_mask, w_in, w_out):
        rows_dev, cols_dev, width = pair.shape
        fits = (
            n_chan == 2
            and rows_dev == SUBLANES
            and 2 * cols_dev == LANES
            and width == LANES
            and width % (4 * n_rows * n_chan) == 0
        )
        if fits:
            return tiled(n_rows, n_chan, pair, block_mask, w_in, w_out)
        return gathered(pair, block_mask, w_in, w_out)

    placed = (P("rows", "chan", None), P(), P(), P())
    return jax.shard_map(
        on_device, mesh=mesh, in_specs=placed, out_specs=P("rows", "chan", None), check_vma=False
    )
```

```python
import functools

import jax
import jax.numpy as jnp
from jax import lax
from jax.experimental import pallas as pl
from jax.experimental.pallas import tpu as pltpu
from jax.sharding import PartitionSpec as P

BLOCK = 128
LANES = 128
SUBLANES = 8
EPS = 1e-05
AXES = ("rows", "chan")
GRANT = pltpu.CompilerParams(vmem_limit_bytes=4 * 1024 * 1024)


def layer_norm(values):
    mean = jnp.mean(values, axis=-1, keepdims=True)
    centered = values - mean
    var = jnp.mean(centered * centered, axis=-1, keepdims=True)
    return centered / jnp.sqrt(var + EPS)


def channel_product(left, piece):
    return jnp.einsum("cik,cjk->cij", left, piece, preferred_element_type=jnp.float32)


def gathered(pair, block_mask, w_in, w_out):
    rows_dev, cols_dev, width = pair.shape
    n_blocks = block_mask.shape[0]
    row_start = lax.axis_index("rows") * rows_dev
    col_start = lax.axis_index("chan") * cols_dev
    row_ids = row_start + lax.broadcasted_iota(jnp.int32, (rows_dev, n_blocks), 0)
    col_ids = col_start + lax.broadcasted_iota(jnp.int32, (cols_dev, n_blocks), 0)
    rows_hot = (
        row_ids // BLOCK == lax.broadcasted_iota(jnp.int32, (rows_dev, n_blocks), 1)
    ).astype(jnp.float32)
    cols_hot = (
        col_ids // BLOCK == lax.broadcasted_iota(jnp.int32, (cols_dev, n_blocks), 1)
    ).astype(jnp.float32)
    mask_float = block_mask.astype(jnp.float32)
    local_mask = jnp.dot(jnp.dot(rows_hot, mask_float), cols_hot.T)[:, :, None]
    normed = layer_norm(pair.astype(jnp.float32)).astype(jnp.bfloat16)
    proj = jnp.dot(normed.reshape(-1, width), w_in, preferred_element_type=jnp.float32).reshape(
        rows_dev, cols_dev, 5 * width
    )
    left = (jax.nn.sigmoid(proj[..., :width]) * proj[..., width : 2 * width] * local_mask).astype(
        jnp.bfloat16
    )
    right = (
        jax.nn.sigmoid(proj[..., 2 * width : 3 * width])
        * proj[..., 3 * width : 4 * width]
        * local_mask
    ).astype(jnp.bfloat16)
    gate = jax.nn.sigmoid(proj[..., 4 * width :])
    left_t = jnp.transpose(left, (2, 0, 1))
    right_t = jnp.transpose(right, (2, 0, 1))
    left_ch, right_ch = (
        lax.all_to_all(left_t, "chan", split_axis=0, concat_axis=2, tiled=True),
        lax.all_to_all(right_t, "chan", split_axis=0, concat_axis=2, tiled=True),
    )
    prod_ch = channel_product(left_ch, lax.all_gather(right_ch, "rows", axis=1, tiled=True))
    prod_back = lax.all_to_all(prod_ch, "chan", split_axis=2, concat_axis=0, tiled=True)
    prod = jnp.transpose(prod_back, (1, 2, 0))
    normed_prod = layer_norm(prod).astype(jnp.bfloat16)
    mixed = jnp.dot(
        normed_prod.reshape(-1, width), w_out, preferred_element_type=jnp.float32
    ).reshape(rows_dev, cols_dev, width)
    return (gate * mixed).astype(jnp.bfloat16)


def dot_t(a, b, contract):
    return lax.dot_general(a, b, ((contract[:1], contract[1:]), ((), ())), preferred_element_type=jnp.float32)


def first_half(shape):
    return lax.broadcasted_iota(jnp.int32, shape, len(shape) - 1) < LANES // 2


def swap(values):
    return pltpu.roll(values, LANES // 2, values.ndim - 1)


def project_kernel(owned, mask_ref, pair_hbm, w_hbm, out_ref, gate_ref, pair_ref, w_ref, parts, sems):
    copies = [
        pltpu.make_async_copy(src, dst, sems.at[at])
        for at, (src, dst) in enumerate(((pair_hbm, pair_ref), (w_hbm, w_ref)))
    ]
    for copy in copies:
        copy.start()
    rows_dev, cols_dev, width = pair_ref.shape
    tokens, half = rows_dev * cols_dev, width // 2
    row_block = lax.axis_index("rows") * rows_dev // BLOCK
    col_block = lax.axis_index("chan") * cols_dev // BLOCK

    across = (width, width)
    diagonal = lax.broadcasted_iota(jnp.int32, across, 0) == lax.broadcasted_iota(jnp.int32, across, 1)
    less_mean = jnp.where(diagonal, 1.0 - 1.0 / width, -1.0 / width).astype(jnp.bfloat16)
    copies[0].wait()
    centered = dot_t(less_mean, pair_ref[...].reshape(tokens, width), (1, 1))
    var = jnp.sum(centered * centered, axis=0, keepdims=True) * (1.0 / width)
    normed = (centered * lax.rsqrt(var + EPS)).astype(jnp.bfloat16)

    copies[1].wait()
    half_mask = 0.5 * mask_ref[row_block, col_block].astype(jnp.float32)
    pick = first_half((half, LANES))
    n_dev, slab = out_ref.shape[0], out_ref.shape[1] // 2
    for side in range(2):
        begin = 2 * side * width
        gates = dot_t(w_ref[:, begin : begin + width], normed, (0, 0))
        values = dot_t(w_ref[:, begin + width : begin + 2 * width], normed, (0, 0))
        held = (jnp.tanh(0.5 * gates) * half_mask + half_mask) * values
        for at in range(tokens // LANES):
            low_c = held[:half, at * LANES : (at + 1) * LANES]
            high_c = held[half:, at * LANES : (at + 1) * LANES]
            parts[side, :, 2 * at, :] = jnp.where(pick, low_c, swap(high_c))
            parts[side, :, 2 * at + 1, :] = jnp.where(pick, swap(low_c), high_c)
        block = parts[side].reshape(n_dev, slab, LANES).astype(jnp.bfloat16)
        for place, group in enumerate(owned):
            out_ref[place, side * slab : (side + 1) * slab, :] = block[group]
    gate = dot_t(w_ref[:, 4 * width :], normed, (0, 0))
    gate_ref[...] = 0.5 * jnp.tanh(0.5 * gate) + 0.5


def product_kernel(n_rows, n_chan, spots, in_ref, out_ref):
    slab = out_ref.shape[1]
    groups = slab // SUBLANES
    tokens = n_rows * SUBLANES

    def side(at):
        values = in_ref[:, at * slab : (at + 1) * slab, :].astype(jnp.float32)
        values = jnp.stack([values[spot] for spot in spots[0]])
        return values.reshape(n_rows, n_chan, groups, SUBLANES, LANES)

    left, right = side(0), side(1)
    pick = first_half((tokens, LANES))
    made = []
    for g in range(groups):
        a = [left[:, x, g].reshape(tokens, LANES) for x in range(n_chan)]
        b = [right[:, x, g].reshape(tokens, LANES) for x in range(n_chan)]
        rows = [
            jnp.concatenate([jnp.where(pick, v, 0.0) for v in a], axis=1),
            jnp.concatenate([jnp.where(pick, 0.0, v) for v in a], axis=1),
        ]
        a = jnp.concatenate(rows, axis=0).astype(jnp.bfloat16)
        b = jnp.concatenate(b, axis=1).astype(jnp.bfloat16)
        prod = dot_t(a, b, (1, 1))
        made.append((prod[:tokens], prod[tokens:]))
    blocks = [
        [jnp.where(pick, low, swap(high)) for low, high in made],
        [jnp.where(pick, swap(low), high) for low, high in made],
    ]
    for x in range(n_chan):
        block = jnp.concatenate([v.reshape(n_rows, SUBLANES, LANES) for v in blocks[x]], axis=1)
        block = block.astype(jnp.bfloat16)
        for row in range(n_rows):
            out_ref[spots[1][row * n_chan + x]] = block[row]


def finish_kernel(prod_ref, gate_ref, w_ref, out_ref, parts):
    n_dev, slab, _ = prod_ref.shape
    rows_dev, cols_dev, width = out_ref.shape
    prod = prod_ref[...].astype(jnp.float32).reshape(n_dev * slab // SUBLANES, SUBLANES, LANES)
    parts[...] = prod
    w = w_ref[...]
    sums = dot_t(w, jnp.ones((width, LANES), jnp.bfloat16), (0, 0))
    total = jnp.sum(prod, axis=0)
    mean = (total + swap(total)) * (1.0 / width)
    centered = prod - mean
    total = jnp.sum(centered * centered, axis=0)
    scale = lax.rsqrt((total + swap(total)) * (1.0 / width) + EPS)

    pick = first_half((width // 2, LANES))
    pick_row = first_half((1, LANES))
    for at in range(rows_dev // 2):
        even, odd = parts[:, 2 * at, :], parts[:, 2 * at + 1, :]
        held = jnp.concatenate(
            [jnp.where(pick, even, swap(odd)), jnp.where(pick, swap(even), odd)], axis=0
        ).astype(jnp.bfloat16)
        row_mean, row_scale = (
            jnp.where(pick_row, v[2 * at : 2 * at + 1], v[2 * at + 1 : 2 * at + 2]) for v in (mean, scale)
        )
        mixed = (dot_t(w, held, (0, 0)) - sums * row_mean) * row_scale
        update = gate_ref[:, at * LANES : (at + 1) * LANES] * mixed
        out_ref[2 * at : 2 * at + 2] = update.astype(jnp.bfloat16).T.reshape(2, cols_dev, width)


def vmem():
    return pl.BlockSpec(memory_space=pltpu.VMEM)


def orders(n_rows, n_chan):
    n_dev = n_rows * n_chan
    quarter = max(n_rows // 4, 1)
    there = [
        (row + at) * n_chan + x
        for x in range(n_chan)
        for at in range(quarter)
        for row in range(n_rows - quarter, -1, -quarter)
    ]
    stride = n_dev // 8 * 2 + 1
    back = [place * stride % n_dev for place in range(n_dev)]
    return there, back


def exchange(values, order):
    return lax.all_to_all(
        values, AXES, split_axis=0, concat_axis=0, axis_index_groups=[order], tiled=True
    )


def tiled(n_rows, n_chan, pair, block_mask, w_in, w_out):
    rows_dev, cols_dev, width = pair.shape
    n_dev = n_rows * n_chan
    groups = width // (2 * n_dev)
    slab = groups * SUBLANES
    there, back = orders(n_rows, n_chan)
    owned = [back.index(device) for device in there]
    spots = [[order.index(device) for device in range(n_dev)] for order in (there, back)]
    sent, gate = pl.pallas_call(
        functools.partial(project_kernel, owned),
        out_shape=(
            jax.ShapeDtypeStruct((n_dev, 2 * slab, LANES), jnp.bfloat16),
            jax.ShapeDtypeStruct((width, rows_dev * cols_dev), jnp.float32),
        ),
        in_specs=[pl.BlockSpec(memory_space=pltpu.SMEM)] + [pl.BlockSpec(memory_space=pltpu.HBM)] * 2,
        out_specs=(vmem(), vmem()),
        scratch_shapes=[
            pltpu.VMEM(pair.shape, pair.dtype),
            pltpu.VMEM(w_in.shape, w_in.dtype),
            pltpu.VMEM((2, width // 2, SUBLANES, LANES), jnp.float32),
            pltpu.SemaphoreType.DMA((2,)),
        ],
        compiler_params=GRANT,
        name="project",
    )(block_mask, *(pltpu.with_memory_space_constraint(v, pltpu.HBM) for v in (pair, w_in)))
    got = exchange(sent, there)
    prod = pl.pallas_call(
        functools.partial(product_kernel, n_rows, n_chan, spots),
        out_shape=jax.ShapeDtypeStruct((n_dev, slab, LANES), jnp.bfloat16),
        in_specs=[vmem()],
        out_specs=vmem(),
        compiler_params=GRANT,
        name="product",
    )(got)
    returned = exchange(prod, back)
    return pl.pallas_call(
        finish_kernel,
        out_shape=jax.ShapeDtypeStruct(pair.shape, jnp.bfloat16),
        in_specs=[vmem()] * 3,
        out_specs=vmem(),
        scratch_shapes=[pltpu.VMEM((width // 2, SUBLANES, LANES), jnp.float32)],
        compiler_params=GRANT,
        name="finish",
    )(returned, gate, w_out)


def solution(mesh):
    n_rows, n_chan = mesh.shape["rows"], mesh.shape["chan"]

    def on_device(pair, block_mask, w_in, w_out):
        rows_dev, cols_dev, width = pair.shape
        fits = (
            n_chan == 2
            and rows_dev == SUBLANES
            and 2 * cols_dev == LANES
            and width == LANES
            and width % (4 * n_rows * n_chan) == 0
        )
        if fits:
            return tiled(n_rows, n_chan, pair, block_mask, w_in, w_out)
        return gathered(pair, block_mask, w_in, w_out)

    placed = (P("rows", "chan", None), P(), P(), P())
    return jax.shard_map(
        on_device, mesh=mesh, in_specs=placed, out_specs=P("rows", "chan", None), check_vma=False
    )
```

```python
import functools

import jax
import jax.numpy as jnp
from jax import lax
from jax.experimental import pallas as pl
from jax.experimental.pallas import tpu as pltpu
from jax.sharding import PartitionSpec as P

BLOCK = 128
LANES = 128
SUBLANES = 8
EPS = 1e-05
AXES = ("rows", "chan")
GRANT = pltpu.CompilerParams(vmem_limit_bytes=4 * 1024 * 1024)


def layer_norm(values):
    mean = jnp.mean(values, axis=-1, keepdims=True)
    centered = values - mean
    var = jnp.mean(centered * centered, axis=-1, keepdims=True)
    return centered / jnp.sqrt(var + EPS)


def channel_product(left, piece):
    return jnp.einsum("cik,cjk->cij", left, piece, preferred_element_type=jnp.float32)


def gathered(pair, block_mask, w_in, w_out):
    rows_dev, cols_dev, width = pair.shape
    n_blocks = block_mask.shape[0]
    row_start = lax.axis_index("rows") * rows_dev
    col_start = lax.axis_index("chan") * cols_dev
    row_ids = row_start + lax.broadcasted_iota(jnp.int32, (rows_dev, n_blocks), 0)
    col_ids = col_start + lax.broadcasted_iota(jnp.int32, (cols_dev, n_blocks), 0)
    rows_hot = (
        row_ids // BLOCK == lax.broadcasted_iota(jnp.int32, (rows_dev, n_blocks), 1)
    ).astype(jnp.float32)
    cols_hot = (
        col_ids // BLOCK == lax.broadcasted_iota(jnp.int32, (cols_dev, n_blocks), 1)
    ).astype(jnp.float32)
    mask_float = block_mask.astype(jnp.float32)
    local_mask = jnp.dot(jnp.dot(rows_hot, mask_float), cols_hot.T)[:, :, None]
    normed = layer_norm(pair.astype(jnp.float32)).astype(jnp.bfloat16)
    proj = jnp.dot(normed.reshape(-1, width), w_in, preferred_element_type=jnp.float32).reshape(
        rows_dev, cols_dev, 5 * width
    )
    left = (jax.nn.sigmoid(proj[..., :width]) * proj[..., width : 2 * width] * local_mask).astype(
        jnp.bfloat16
    )
    right = (
        jax.nn.sigmoid(proj[..., 2 * width : 3 * width])
        * proj[..., 3 * width : 4 * width]
        * local_mask
    ).astype(jnp.bfloat16)
    gate = jax.nn.sigmoid(proj[..., 4 * width :])
    left_t = jnp.transpose(left, (2, 0, 1))
    right_t = jnp.transpose(right, (2, 0, 1))
    left_ch, right_ch = (
        lax.all_to_all(left_t, "chan", split_axis=0, concat_axis=2, tiled=True),
        lax.all_to_all(right_t, "chan", split_axis=0, concat_axis=2, tiled=True),
    )
    prod_ch = channel_product(left_ch, lax.all_gather(right_ch, "rows", axis=1, tiled=True))
    prod_back = lax.all_to_all(prod_ch, "chan", split_axis=2, concat_axis=0, tiled=True)
    prod = jnp.transpose(prod_back, (1, 2, 0))
    normed_prod = layer_norm(prod).astype(jnp.bfloat16)
    mixed = jnp.dot(
        normed_prod.reshape(-1, width), w_out, preferred_element_type=jnp.float32
    ).reshape(rows_dev, cols_dev, width)
    return (gate * mixed).astype(jnp.bfloat16)


def dot_t(a, b, contract):
    return lax.dot_general(a, b, ((contract[:1], contract[1:]), ((), ())), preferred_element_type=jnp.float32)


def first_half(shape):
    return lax.broadcasted_iota(jnp.int32, shape, len(shape) - 1) < LANES // 2


def swap(values):
    return pltpu.roll(values, LANES // 2, values.ndim - 1)


def project_kernel(owned, mask_ref, pair_hbm, w_hbm, out_ref, gate_ref, pair_ref, w_ref, sems):
    copies = [
        pltpu.make_async_copy(src, dst, sems.at[at])
        for at, (src, dst) in enumerate(((pair_hbm, pair_ref), (w_hbm, w_ref)))
    ]
    for copy in copies:
        copy.start()
    rows_dev, cols_dev, width = pair_ref.shape
    tokens, half = rows_dev * cols_dev, width // 2
    row_block = lax.axis_index("rows") * rows_dev // BLOCK
    col_block = lax.axis_index("chan") * cols_dev // BLOCK

    across = (width, width)
    diagonal = lax.broadcasted_iota(jnp.int32, across, 0) == lax.broadcasted_iota(jnp.int32, across, 1)
    less_mean = jnp.where(diagonal, 1.0 - 1.0 / width, -1.0 / width).astype(jnp.bfloat16)
    copies[0].wait()
    centered = dot_t(less_mean, pair_ref[...].reshape(tokens, width), (1, 1))
    var = jnp.sum(centered * centered, axis=0, keepdims=True) * (1.0 / width)
    normed = (centered * lax.rsqrt(var + EPS)).astype(jnp.bfloat16)

    copies[1].wait()
    half_mask = 0.5 * mask_ref[row_block, col_block].astype(jnp.float32)
    pick = first_half((half, LANES))
    n_dev, slab = out_ref.shape[0], out_ref.shape[1] // 2
    for side in range(2):
        begin = 2 * side * width
        gates = dot_t(w_ref[:, begin : begin + width], normed, (0, 0))
        values = dot_t(w_ref[:, begin + width : begin + 2 * width], normed, (0, 0))
        held = (jnp.tanh(0.5 * gates) * half_mask + half_mask) * values
        by_row = []
        for at in range(tokens // LANES):
            low_c = held[:half, at * LANES : (at + 1) * LANES]
            high_c = held[half:, at * LANES : (at + 1) * LANES]
            by_row.append(jnp.where(pick, low_c, swap(high_c)))
            by_row.append(jnp.where(pick, swap(low_c), high_c))
        block = pltpu.einshape("icl->cil", jnp.stack(by_row))
        block = block.reshape(n_dev, slab, LANES).astype(jnp.bfloat16)
        for place, group in enumerate(owned):
            out_ref[place, side * slab : (side + 1) * slab, :] = block[group]
    gate = dot_t(w_ref[:, 4 * width :], normed, (0, 0))
    gate_ref[...] = 0.5 * jnp.tanh(0.5 * gate) + 0.5


def product_kernel(n_rows, n_chan, spots, in_ref, out_ref):
    slab = out_ref.shape[1]
    groups = slab // SUBLANES
    tokens = n_rows * SUBLANES

    def side(at):
        values = in_ref[:, at * slab : (at + 1) * slab, :].astype(jnp.float32)
        values = jnp.stack([values[spot] for spot in spots[0]])
        return values.reshape(n_rows, n_chan, groups, SUBLANES, LANES)

    left, right = side(0), side(1)
    pick = first_half((tokens, LANES))
    made = []
    for g in range(groups):
        a = [left[:, x, g].reshape(tokens, LANES) for x in range(n_chan)]
        b = [right[:, x, g].reshape(tokens, LANES) for x in range(n_chan)]
        rows = [
            jnp.concatenate([jnp.where(pick, v, 0.0) for v in a], axis=1),
            jnp.concatenate([jnp.where(pick, 0.0, v) for v in a], axis=1),
        ]
        a = jnp.concatenate(rows, axis=0).astype(jnp.bfloat16)
        b = jnp.concatenate(b, axis=1).astype(jnp.bfloat16)
        prod = dot_t(a, b, (1, 1))
        made.append((prod[:tokens], prod[tokens:]))
    blocks = [
        [jnp.where(pick, low, swap(high)) for low, high in made],
        [jnp.where(pick, swap(low), high) for low, high in made],
    ]
    for x in range(n_chan):
        block = jnp.concatenate([v.reshape(n_rows, SUBLANES, LANES) for v in blocks[x]], axis=1)
        block = block.astype(jnp.bfloat16)
        for row in range(n_rows):
            out_ref[spots[1][row * n_chan + x]] = block[row]


def finish_kernel(prod_ref, gate_ref, w_ref, out_ref):
    n_dev, slab, _ = prod_ref.shape
    rows_dev, cols_dev, width = out_ref.shape
    prod = prod_ref[...].astype(jnp.float32).reshape(n_dev * slab // SUBLANES, SUBLANES, LANES)
    by_row = pltpu.einshape("cil->icl", prod)
    w = w_ref[...]
    sums = dot_t(w, jnp.ones((width, LANES), jnp.bfloat16), (0, 0))
    total = jnp.sum(prod, axis=0)
    mean = (total + swap(total)) * (1.0 / width)
    centered = prod - mean
    total = jnp.sum(centered * centered, axis=0)
    scale = lax.rsqrt((total + swap(total)) * (1.0 / width) + EPS)

    pick = first_half((width // 2, LANES))
    pick_row = first_half((1, LANES))
    for at in range(rows_dev // 2):
        even, odd = by_row[2 * at], by_row[2 * at + 1]
        held = jnp.concatenate(
            [jnp.where(pick, even, swap(odd)), jnp.where(pick, swap(even), odd)], axis=0
        ).astype(jnp.bfloat16)
        row_mean, row_scale = (
            jnp.where(pick_row, v[2 * at : 2 * at + 1], v[2 * at + 1 : 2 * at + 2]) for v in (mean, scale)
        )
        mixed = (dot_t(w, held, (0, 0)) - sums * row_mean) * row_scale
        update = gate_ref[:, at * LANES : (at + 1) * LANES] * mixed
        out_ref[2 * at : 2 * at + 2] = update.astype(jnp.bfloat16).T.reshape(2, cols_dev, width)


def vmem():
    return pl.BlockSpec(memory_space=pltpu.VMEM)


def orders(n_rows, n_chan):
    n_dev = n_rows * n_chan
    quarter = max(n_rows // 4, 1)
    there = [
        (row + at) * n_chan + x
        for x in range(n_chan)
        for at in range(quarter)
        for row in range(n_rows - quarter, -1, -quarter)
    ]
    stride = n_dev // 8 * 2 + 1
    back = [place * stride % n_dev for place in range(n_dev)]
    return there, back


def exchange(values, order):
    return lax.all_to_all(
        values, AXES, split_axis=0, concat_axis=0, axis_index_groups=[order], tiled=True
    )


def tiled(n_rows, n_chan, pair, block_mask, w_in, w_out):
    rows_dev, cols_dev, width = pair.shape
    n_dev = n_rows * n_chan
    groups = width // (2 * n_dev)
    slab = groups * SUBLANES
    there, back = orders(n_rows, n_chan)
    owned = [back.index(device) for device in there]
    spots = [[order.index(device) for device in range(n_dev)] for order in (there, back)]
    sent, gate = pl.pallas_call(
        functools.partial(project_kernel, owned),
        out_shape=(
            jax.ShapeDtypeStruct((n_dev, 2 * slab, LANES), jnp.bfloat16),
            jax.ShapeDtypeStruct((width, rows_dev * cols_dev), jnp.float32),
        ),
        in_specs=[pl.BlockSpec(memory_space=pltpu.SMEM)] + [pl.BlockSpec(memory_space=pltpu.HBM)] * 2,
        out_specs=(vmem(), vmem()),
        scratch_shapes=[
            pltpu.VMEM(pair.shape, pair.dtype),
            pltpu.VMEM(w_in.shape, w_in.dtype),
            pltpu.SemaphoreType.DMA((2,)),
        ],
        compiler_params=GRANT,
        name="project",
    )(block_mask, *(pltpu.with_memory_space_constraint(v, pltpu.HBM) for v in (pair, w_in)))
    got = exchange(sent, there)
    prod = pl.pallas_call(
        functools.partial(product_kernel, n_rows, n_chan, spots),
        out_shape=jax.ShapeDtypeStruct((n_dev, slab, LANES), jnp.bfloat16),
        in_specs=[vmem()],
        out_specs=vmem(),
        compiler_params=GRANT,
        name="product",
    )(got)
    returned = exchange(prod, back)
    return pl.pallas_call(
        finish_kernel,
        out_shape=jax.ShapeDtypeStruct(pair.shape, jnp.bfloat16),
        in_specs=[vmem()] * 3,
        out_specs=vmem(),
        compiler_params=GRANT,
        name="finish",
    )(returned, gate, w_out)


def solution(mesh):
    n_rows, n_chan = mesh.shape["rows"], mesh.shape["chan"]

    def on_device(pair, block_mask, w_in, w_out):
        rows_dev, cols_dev, width = pair.shape
        fits = (
            n_chan == 2
            and rows_dev == SUBLANES
            and 2 * cols_dev == LANES
            and width == LANES
            and width % (4 * n_rows * n_chan) == 0
        )
        if fits:
            return tiled(n_rows, n_chan, pair, block_mask, w_in, w_out)
        return gathered(pair, block_mask, w_in, w_out)

    placed = (P("rows", "chan", None), P(), P(), P())
    return jax.shard_map(
        on_device, mesh=mesh, in_specs=placed, out_specs=P("rows", "chan", None), check_vma=False
    )
```

```python
import functools

import jax
import jax.numpy as jnp
from jax import lax
from jax.experimental import pallas as pl
from jax.experimental.pallas import tpu as pltpu
from jax.sharding import PartitionSpec as P

BLOCK = 128
LANES = 128
SUBLANES = 8
EPS = 1e-05
AXES = ("rows", "chan")
GRANT = pltpu.CompilerParams(vmem_limit_bytes=4 * 1024 * 1024)


def layer_norm(values):
    mean = jnp.mean(values, axis=-1, keepdims=True)
    centered = values - mean
    var = jnp.mean(centered * centered, axis=-1, keepdims=True)
    return centered / jnp.sqrt(var + EPS)


def channel_product(left, piece):
    return jnp.einsum("cik,cjk->cij", left, piece, preferred_element_type=jnp.float32)


def gathered(pair, block_mask, w_in, w_out):
    rows_dev, cols_dev, width = pair.shape
    n_blocks = block_mask.shape[0]
    row_start = lax.axis_index("rows") * rows_dev
    col_start = lax.axis_index("chan") * cols_dev
    row_ids = row_start + lax.broadcasted_iota(jnp.int32, (rows_dev, n_blocks), 0)
    col_ids = col_start + lax.broadcasted_iota(jnp.int32, (cols_dev, n_blocks), 0)
    rows_hot = (
        row_ids // BLOCK == lax.broadcasted_iota(jnp.int32, (rows_dev, n_blocks), 1)
    ).astype(jnp.float32)
    cols_hot = (
        col_ids // BLOCK == lax.broadcasted_iota(jnp.int32, (cols_dev, n_blocks), 1)
    ).astype(jnp.float32)
    mask_float = block_mask.astype(jnp.float32)
    local_mask = jnp.dot(jnp.dot(rows_hot, mask_float), cols_hot.T)[:, :, None]
    normed = layer_norm(pair.astype(jnp.float32)).astype(jnp.bfloat16)
    proj = jnp.dot(normed.reshape(-1, width), w_in, preferred_element_type=jnp.float32).reshape(
        rows_dev, cols_dev, 5 * width
    )
    left = (jax.nn.sigmoid(proj[..., :width]) * proj[..., width : 2 * width] * local_mask).astype(
        jnp.bfloat16
    )
    right = (
        jax.nn.sigmoid(proj[..., 2 * width : 3 * width])
        * proj[..., 3 * width : 4 * width]
        * local_mask
    ).astype(jnp.bfloat16)
    gate = jax.nn.sigmoid(proj[..., 4 * width :])
    left_t = jnp.transpose(left, (2, 0, 1))
    right_t = jnp.transpose(right, (2, 0, 1))
    left_ch, right_ch = (
        lax.all_to_all(left_t, "chan", split_axis=0, concat_axis=2, tiled=True),
        lax.all_to_all(right_t, "chan", split_axis=0, concat_axis=2, tiled=True),
    )
    prod_ch = channel_product(left_ch, lax.all_gather(right_ch, "rows", axis=1, tiled=True))
    prod_back = lax.all_to_all(prod_ch, "chan", split_axis=2, concat_axis=0, tiled=True)
    prod = jnp.transpose(prod_back, (1, 2, 0))
    normed_prod = layer_norm(prod).astype(jnp.bfloat16)
    mixed = jnp.dot(
        normed_prod.reshape(-1, width), w_out, preferred_element_type=jnp.float32
    ).reshape(rows_dev, cols_dev, width)
    return (gate * mixed).astype(jnp.bfloat16)


def dot_t(a, b, contract):
    return lax.dot_general(a, b, ((contract[:1], contract[1:]), ((), ())), preferred_element_type=jnp.float32)


def first_half(shape):
    return lax.broadcasted_iota(jnp.int32, shape, len(shape) - 1) < LANES // 2


def swap(values):
    return pltpu.roll(values, LANES // 2, values.ndim - 1)


def project_kernel(owned, mask_ref, pair_hbm, w_hbm, out_ref, gate_ref, pair_ref, w_ref, sems):
    copies = [
        pltpu.make_async_copy(src, dst, sems.at[at])
        for at, (src, dst) in enumerate(((pair_hbm, pair_ref), (w_hbm, w_ref)))
    ]
    for copy in copies:
        copy.start()
    rows_dev, cols_dev, width = pair_ref.shape
    tokens, half = rows_dev * cols_dev, width // 2
    row_block = lax.axis_index("rows") * rows_dev // BLOCK
    col_block = lax.axis_index("chan") * cols_dev // BLOCK

    across = (width, width)
    diagonal = lax.broadcasted_iota(jnp.int32, across, 0) == lax.broadcasted_iota(jnp.int32, across, 1)
    less_mean = jnp.where(diagonal, 1.0 - 1.0 / width, -1.0 / width).astype(jnp.bfloat16)
    copies[0].wait()
    centered = dot_t(less_mean, pair_ref[...].reshape(tokens, width), (1, 1))
    var = jnp.sum(centered * centered, axis=0, keepdims=True) * (1.0 / width)
    normed = (centered * lax.rsqrt(var + EPS)).astype(jnp.bfloat16)

    copies[1].wait()
    half_mask = 0.5 * mask_ref[row_block, col_block].astype(jnp.float32)
    pick = first_half((half, LANES))
    n_dev, slab = out_ref.shape[0], out_ref.shape[1] // 2
    for side in range(2):
        begin = 2 * side * width
        gates = dot_t(w_ref[:, begin : begin + width], normed, (0, 0))
        values = dot_t(w_ref[:, begin + width : begin + 2 * width], normed, (0, 0))
        held = (jnp.tanh(0.5 * gates) * half_mask + half_mask) * values
        held = held.astype(jnp.bfloat16)
        by_row = []
        for at in range(tokens // LANES):
            low_c = held[:half, at * LANES : (at + 1) * LANES]
            high_c = held[half:, at * LANES : (at + 1) * LANES]
            by_row.append(jnp.where(pick, low_c, swap(high_c)))
            by_row.append(jnp.where(pick, swap(low_c), high_c))
        block = pltpu.einshape("icl->cil", jnp.stack(by_row))
        block = block.reshape(n_dev, slab, LANES)
        for place, group in enumerate(owned):
            out_ref[place, side * slab : (side + 1) * slab, :] = block[group]
    gate = dot_t(w_ref[:, 4 * width :], normed, (0, 0))
    gate_ref[...] = 0.5 * jnp.tanh(0.5 * gate) + 0.5


def product_kernel(n_rows, n_chan, spots, in_ref, out_ref):
    slab = out_ref.shape[1]
    groups = slab // SUBLANES
    tokens = n_rows * SUBLANES

    def side(at):
        values = in_ref[:, at * slab : (at + 1) * slab, :].astype(jnp.float32)
        values = jnp.stack([values[spot] for spot in spots[0]])
        return values.reshape(n_rows, n_chan, groups, SUBLANES, LANES)

    left, right = side(0), side(1)
    pick = first_half((tokens, LANES))
    made = []
    for g in range(groups):
        a = [left[:, x, g].reshape(tokens, LANES) for x in range(n_chan)]
        b = [right[:, x, g].reshape(tokens, LANES) for x in range(n_chan)]
        rows = [
            jnp.concatenate([jnp.where(pick, v, 0.0) for v in a], axis=1),
            jnp.concatenate([jnp.where(pick, 0.0, v) for v in a], axis=1),
        ]
        a = jnp.concatenate(rows, axis=0).astype(jnp.bfloat16)
        b = jnp.concatenate(b, axis=1).astype(jnp.bfloat16)
        prod = dot_t(a, b, (1, 1))
        made.append((prod[:tokens], prod[tokens:]))
    blocks = [
        [jnp.where(pick, low, swap(high)) for low, high in made],
        [jnp.where(pick, swap(low), high) for low, high in made],
    ]
    for x in range(n_chan):
        block = jnp.concatenate([v.reshape(n_rows, SUBLANES, LANES) for v in blocks[x]], axis=1)
        block = block.astype(jnp.bfloat16)
        for row in range(n_rows):
            out_ref[spots[1][row * n_chan + x]] = block[row]


def finish_kernel(prod_ref, gate_ref, w_ref, out_ref):
    n_dev, slab, _ = prod_ref.shape
    rows_dev, cols_dev, width = out_ref.shape
    prod = prod_ref[...].astype(jnp.float32).reshape(n_dev * slab // SUBLANES, SUBLANES, LANES)
    by_row = pltpu.einshape("cil->icl", prod)
    w = w_ref[...]
    sums = dot_t(w, jnp.ones((width, LANES), jnp.bfloat16), (0, 0))
    total = jnp.sum(prod, axis=0)
    mean = (total + swap(total)) * (1.0 / width)
    centered = prod - mean
    total = jnp.sum(centered * centered, axis=0)
    scale = lax.rsqrt((total + swap(total)) * (1.0 / width) + EPS)

    pick = first_half((width // 2, LANES))
    pick_row = first_half((1, LANES))
    for at in range(rows_dev // 2):
        even, odd = by_row[2 * at], by_row[2 * at + 1]
        held = jnp.concatenate(
            [jnp.where(pick, even, swap(odd)), jnp.where(pick, swap(even), odd)], axis=0
        ).astype(jnp.bfloat16)
        row_mean, row_scale = (
            jnp.where(pick_row, v[2 * at : 2 * at + 1], v[2 * at + 1 : 2 * at + 2]) for v in (mean, scale)
        )
        mixed = (dot_t(w, held, (0, 0)) - sums * row_mean) * row_scale
        update = gate_ref[:, at * LANES : (at + 1) * LANES] * mixed
        out_ref[2 * at : 2 * at + 2] = update.astype(jnp.bfloat16).T.reshape(2, cols_dev, width)


def vmem():
    return pl.BlockSpec(memory_space=pltpu.VMEM)


def orders(n_rows, n_chan):
    n_dev = n_rows * n_chan
    quarter = max(n_rows // 4, 1)
    there = [
        (row + at) * n_chan + x
        for x in range(n_chan)
        for at in range(quarter)
        for row in range(n_rows - quarter, -1, -quarter)
    ]
    stride = n_dev // 8 * 2 + 1
    back = [place * stride % n_dev for place in range(n_dev)]
    return there, back


def exchange(values, order):
    return lax.all_to_all(
        values, AXES, split_axis=0, concat_axis=0, axis_index_groups=[order], tiled=True
    )


def tiled(n_rows, n_chan, pair, block_mask, w_in, w_out):
    rows_dev, cols_dev, width = pair.shape
    n_dev = n_rows * n_chan
    groups = width // (2 * n_dev)
    slab = groups * SUBLANES
    there, back = orders(n_rows, n_chan)
    owned = [back.index(device) for device in there]
    spots = [[order.index(device) for device in range(n_dev)] for order in (there, back)]
    sent, gate = pl.pallas_call(
        functools.partial(project_kernel, owned),
        out_shape=(
            jax.ShapeDtypeStruct((n_dev, 2 * slab, LANES), jnp.bfloat16),
            jax.ShapeDtypeStruct((width, rows_dev * cols_dev), jnp.float32),
        ),
        in_specs=[pl.BlockSpec(memory_space=pltpu.SMEM)] + [pl.BlockSpec(memory_space=pltpu.HBM)] * 2,
        out_specs=(vmem(), vmem()),
        scratch_shapes=[
            pltpu.VMEM(pair.shape, pair.dtype),
            pltpu.VMEM(w_in.shape, w_in.dtype),
            pltpu.SemaphoreType.DMA((2,)),
        ],
        compiler_params=GRANT,
        name="project",
    )(block_mask, *(pltpu.with_memory_space_constraint(v, pltpu.HBM) for v in (pair, w_in)))
    got = exchange(sent, there)
    prod = pl.pallas_call(
        functools.partial(product_kernel, n_rows, n_chan, spots),
        out_shape=jax.ShapeDtypeStruct((n_dev, slab, LANES), jnp.bfloat16),
        in_specs=[vmem()],
        out_specs=vmem(),
        compiler_params=GRANT,
        name="product",
    )(got)
    returned = exchange(prod, back)
    return pl.pallas_call(
        finish_kernel,
        out_shape=jax.ShapeDtypeStruct(pair.shape, jnp.bfloat16),
        in_specs=[vmem()] * 3,
        out_specs=vmem(),
        compiler_params=GRANT,
        name="finish",
    )(returned, gate, w_out)


def solution(mesh):
    n_rows, n_chan = mesh.shape["rows"], mesh.shape["chan"]

    def on_device(pair, block_mask, w_in, w_out):
        rows_dev, cols_dev, width = pair.shape
        fits = (
            n_chan == 2
            and rows_dev == SUBLANES
            and 2 * cols_dev == LANES
            and width == LANES
            and width % (4 * n_rows * n_chan) == 0
        )
        if fits:
            return tiled(n_rows, n_chan, pair, block_mask, w_in, w_out)
        return gathered(pair, block_mask, w_in, w_out)

    placed = (P("rows", "chan", None), P(), P(), P())
    return jax.shard_map(
        on_device, mesh=mesh, in_specs=placed, out_specs=P("rows", "chan", None), check_vma=False
    )
```
